512 devices in a mesh: grp: 4 (over y), dev: 128 (over z, x, core).
Axes of the slice: x: 4, y: 4, z: 16, core: 2. Of those that a mesh axis runs over, the one named last changes fastest.
Arguments:
- embeddings: bfloat16 [131072, 768], P(('grp', 'dev')), parts along dimension 0, may hold values from -80 to 80, as said below
- block_ids: int32 [131072], P(('grp', 'dev')), parts along dimension 0, may hold values from 0 to 127, as said below
Outputs:
- maxima: float32 [131072], P(('grp', 'dev')), parts along dimension 0
The draws below stay inside these ranges and needn't reach their ends.
There are 4 independent parts, one for each index of `grp`. The reference program is written for one: setup_inputs(seed, part) draws one part's arguments, and reference() takes and returns one part's arrays. A program takes and returns all parts, laid end to end along the dimension named above; each array names one. Nothing has to cross between parts.
Inputs may be any that keep to these rules, and one draw needn't show every extreme that they name: `block_ids`: at most 4 rows of one device name one block; every block is named by at least one row of every device; in every draw one block is named by 4 rows of every device. `embeddings`: no row is zero.
All inputs are finite; a program needn't handle non-finite values.
Results may differ from the reference program's by a relative error of at most 0.00049.
Values may be sent and summed in bfloat16 or wider, within the bound.
No kernel may reach another device: no remote copies, remote signals or barrier semaphores. Data moves between devices by JAX's collectives and lax.ppermute only.
A program may use at most 64 MiB of HBM per device.

```python
import math
import jax
import jax.numpy as jnp
from jax import lax

E = 768
ROWS_DEV = 256
CLUSTER_SLOTS = 512
CAPB = 4
ROWS = 32768
N_DEV = 128


def block_layout(key):
    key = jax.random.fold_in(key, 101)
    key_hot, key_level, key_rows = jax.random.split(key, 3)
    busiest_block = jax.random.randint(key_hot, (), 0, N_DEV)
    block_of_slot = jnp.arange(CLUSTER_SLOTS, dtype=jnp.int32) // CAPB
    rank_of_slot = jnp.arange(CLUSTER_SLOTS, dtype=jnp.int32) % CAPB
    tier_values = jax.random.randint(key_level, (N_DEV,), 0, 4)
    extra_credit = tier_values[block_of_slot] * 524288 + jnp.where(rank_of_slot == 0, 8388608, 0) + jnp.where(block_of_slot == busiest_block, 16777216, 0)

    def one_device(device):
        device_key = jax.random.fold_in(key_rows, device)
        key_jitter, key_order = jax.random.split(device_key)
        precedence = jax.random.randint(key_jitter, (CLUSTER_SLOTS,), 0, 1048576) + extra_credit
        chosen = jnp.argsort(-precedence, stable=True)[:ROWS_DEV]
        return block_of_slot[jax.random.permutation(key_order, chosen)]
    return jax.vmap(one_device)(jnp.arange(N_DEV)).reshape(ROWS_DEV * N_DEV).astype(jnp.int32)


def twin_rows(key, blocks):
    key_pick, key_side, key_twin = jax.random.split(key, 3)
    counts = jax.ops.segment_sum(jnp.ones((ROWS,), jnp.int32), blocks, num_segments=N_DEV)
    starts = jnp.cumsum(counts) - counts
    order = jnp.argsort(blocks, stable=True).astype(jnp.int32)
    flip = jax.random.randint(key_side, (ROWS,), 0, 5) < 3
    target_block = jnp.where(flip, blocks ^ 1, blocks)
    pick = jax.random.randint(key_twin, (ROWS,), 0, 1048576) % counts[target_block]
    twin = order[starts[target_block] + pick]
    planted = jax.random.randint(key_pick, (ROWS,), 0, 20) < 3
    return (twin, planted)


def draw_block_ids(key, part):
    return block_layout(key)


def draw_embeddings(key, part):
    blocks = block_layout(key)
    key = jax.random.fold_in(key, 5)
    keys = jax.random.split(key, 8)
    key_center, key_mix, key_jitter, key_scale, key_copy, key_spread, key_dup, key_size = keys
    twin, planted = twin_rows(key_copy, blocks)
    cluster = blocks // 2
    centers = jax.random.truncated_normal(key_center, -4.0, 4.0, (N_DEV // 2, E), jnp.float32)
    spread = jnp.exp(jax.random.uniform(key_spread, (ROWS, 1), jnp.float32, math.log(0.045), math.log(0.33)))
    size = jnp.exp(jax.random.uniform(key_size, (ROWS, 1), jnp.float32, math.log(0.7), math.log(1.4)))
    mixing = jnp.exp(jax.random.uniform(key_mix, (ROWS, 1), jnp.float32, math.log(0.15), math.log(3.0)))
    noise = jax.random.truncated_normal(key_jitter, -4.0, 4.0, (ROWS, E), jnp.float32)
    dup_noise = jax.random.truncated_normal(key_dup, -4.0, 4.0, (ROWS, E), jnp.float32)
    base = centers[cluster] * mixing + noise
    sigma = spread * jnp.sqrt(1.0 + mixing[twin] * mixing[twin])
    duplicate = (base[twin] + sigma * dup_noise) * size
    values = jnp.where(planted[:, None], duplicate, base)
    return jnp.clip(values, -79.0, 79.0).astype(jnp.bfloat16)


def setup_inputs(seed: int = 0, part: int = 0) -> dict:
    splits = jax.random.split(jax.random.key(seed), 3)
    part_keys = jax.random.split(jax.random.fold_in(splits[2], part), 3)
    return {
        "embeddings": draw_embeddings(jax.random.fold_in(jax.random.fold_in(splits[2], part), 71), part),
        "block_ids": draw_block_ids(jax.random.fold_in(jax.random.fold_in(splits[2], part), 71), part),
    }


def reference(embeddings, block_ids):
    values = embeddings.astype(jnp.float32)
    unit_rows = (values * lax.rsqrt(lax.optimization_barrier(jnp.sum(values * values, axis=1, keepdims=True)) + 1e-06)).astype(jnp.bfloat16)
    blocks = block_ids.reshape(N_DEV, ROWS_DEV)
    onehot = (blocks[:, :, None] == jnp.arange(N_DEV, dtype=jnp.int32)[None, None, :]).astype(jnp.int32)
    row_rank = lax.optimization_barrier(jnp.sum(jnp.cumsum(onehot, axis=1) * onehot, axis=2)) - 1
    source = jnp.arange(N_DEV, dtype=jnp.int32)[:, None]
    position = (source * CAPB + row_rank).reshape(ROWS_DEV * N_DEV).astype(jnp.int32)
    padded = jnp.zeros((N_DEV, CLUSTER_SLOTS, E), jnp.bfloat16).at[block_ids, position].set(unit_rows)
    pairs = padded.reshape(N_DEV // 2, 2 * CLUSTER_SLOTS, E)

    def cluster_max(members):
        members_wide = members.astype(jnp.float32)
        present = jnp.any(members != 0, axis=1)
        scores = jnp.dot(members_wide, members_wide.T, precision=lax.Precision.HIGHEST)
        indices = jnp.arange(2 * CLUSTER_SLOTS, dtype=jnp.int32)
        allowed = present[None, :] & (indices[:, None] != indices[None, :])
        return lax.optimization_barrier(jnp.max(jnp.where(allowed, scores, -jnp.inf), axis=1))
    cluster_best = lax.map(cluster_max, pairs).reshape(N_DEV, CLUSTER_SLOTS)
    return cluster_best[block_ids, position]
```

```python
import functools

import jax
import jax.numpy as jnp
from jax import lax
from jax.experimental import pallas as pl
from jax.experimental.pallas import tpu as pltpu
from jax.sharding import PartitionSpec as P

CAPACITY = 8
LANES = 128
LOWEST = -1e30
VMEM_BYTES = 16 * 1024 * 1024


def iota(shape, axis):
    return lax.broadcasted_iota(jnp.int32, shape, axis)


def place_kernel(ids_ref, rows_ref, placed_ref, slot_ref):
    count = rows_ref.shape[0]
    slots = placed_ref.shape[0]
    cluster = jnp.broadcast_to(ids_ref[...] // 2, (count, count))
    above, here = iota((count, count), 0), iota((count, count), 1)
    cluster_above = jnp.sum(jnp.where(above == here, cluster, 0), axis=1, keepdims=True)
    earlier = (cluster_above == cluster) & (above < here)
    rank = jnp.sum(earlier.astype(jnp.int32), axis=0, keepdims=True)
    slot = cluster[:1] * CAPACITY + rank
    slot_ref[...] = slot
    values = rows_ref[...].astype(jnp.float32)
    norm = lax.rsqrt(jnp.sum(values * values, axis=1, keepdims=True) + 1e-06)
    unit = (values * norm).astype(jnp.bfloat16)
    onehot = (iota((slots, count), 0) == slot).astype(jnp.float32).astype(jnp.bfloat16)
    placed_ref[...] = jnp.dot(onehot, unit, preferred_element_type=jnp.float32).astype(
        jnp.bfloat16
    )


def present(rows):
    return jnp.max(jnp.abs(rows).astype(jnp.float32), axis=1, keepdims=True) > 0


def scores_of(others, own):
    return lax.dot_general(
        others, own, (((1,), (1,)), ((), ())), preferred_element_type=jnp.float32
    )


def own_kernel(own_ref, best_ref):
    own = own_ref[...]
    scores = scores_of(own, own)
    allowed = present(own) & (iota(scores.shape, 0) != iota(scores.shape, 1))
    best_ref[...] = jnp.max(jnp.where(allowed, scores, LOWEST), axis=0, keepdims=True)


def cross_kernel(own_ref, other_ref, best_ref, message_ref):
    own, other = own_ref[...], other_ref[...]
    scores = jnp.where(present(other), scores_of(other, own), LOWEST)
    best = jnp.maximum(best_ref[...], jnp.max(scores, axis=0, keepdims=True))
    shape = message_ref.shape
    source, lane = iota(shape, 0), iota(shape, 1)
    message = jnp.zeros(shape, jnp.float32)
    per_part = LANES // CAPACITY
    for part in range(best.shape[1] // LANES):
        mine = source == part * per_part + lane // CAPACITY
        message = jnp.where(mine, best[:, part * LANES : (part + 1) * LANES], message)
    message_ref[...] = message


def pick_kernel(slot_ref, answers_ref, out_ref):
    slot = slot_ref[...]
    answers = answers_ref[...]
    count = slot.shape[1]
    onehot = (iota((answers.shape[0], count), 0) == slot // CAPACITY).astype(jnp.float32)
    found = lax.dot_general(
        answers,
        onehot,
        (((0,), (0,)), ((), ())),
        precision=lax.Precision.HIGHEST,
        preferred_element_type=jnp.float32,
    )
    mine = iota(found.shape, 0) % CAPACITY == slot % CAPACITY
    out_ref[...] = jnp.sum(jnp.where(mine, found, 0.0), axis=0, keepdims=True)


def call(kernel, outs, flops, *args):
    whole = pl.BlockSpec(memory_space=pltpu.VMEM)
    moved = sum(a.size * a.dtype.itemsize for a in args)
    return pl.pallas_call(
        kernel,
        out_shape=outs,
        in_specs=[whole] * len(args),
        out_specs=jax.tree.map(lambda _: whole, outs),
        compiler_params=pltpu.CompilerParams(vmem_limit_bytes=VMEM_BYTES),
        cost_estimate=pl.CostEstimate(flops=flops, bytes_accessed=moved, transcendentals=0),
    )(*args)


def body(embeddings, block_ids):
    count, width = embeddings.shape
    devices = lax.axis_size("dev")
    chips = devices // 2
    slots = chips * CAPACITY
    same_core = [[2 * chip + core for chip in range(chips)] for core in range(2)]
    exchange = functools.partial(
        lax.all_to_all,
        axis_name="dev",
        split_axis=0,
        concat_axis=0,
        axis_index_groups=same_core,
        tiled=True,
    )
    row = jax.ShapeDtypeStruct
    placed, slot = call(
        place_kernel,
        (row((slots, width), jnp.bfloat16), row((1, count), jnp.int32)),
        2 * slots * count * width,
        block_ids.reshape(1, count),
        embeddings,
    )
    own = exchange(placed.reshape(chips, CAPACITY, width)).reshape(slots, width)
    other = lax.ppermute(own, "dev", [(d, d ^ 1) for d in range(devices)])
    flops = 2 * slots * slots * width
    best = call(own_kernel, row((1, slots), jnp.float32), flops, own)
    message = call(cross_kernel, row((chips, LANES), jnp.float32), flops, own, other, best)
    answers = exchange(message.reshape(chips, 1, LANES)).reshape(chips, LANES)
    out = call(pick_kernel, row((1, count), jnp.float32), 2 * chips * LANES * count, slot, answers)
    return out.reshape(count)


def solution(mesh):
    placed = (P(("grp", "dev"), None), P(("grp", "dev")))
    return jax.shard_map(
        body, mesh=mesh, in_specs=placed, out_specs=P(("grp", "dev")), check_vma=False
    )
```

```python
import functools

import jax
import jax.numpy as jnp
from jax import lax
from jax.experimental import pallas as pl
from jax.experimental.pallas import tpu as pltpu
from jax.sharding import PartitionSpec as P

CAPACITY = 8
LANES = 128
LOWEST = -1e30
ROWS_FIRST = 42
ANSWERS_FIRST = 34
SLOT_COST = 2_000_000_000
VMEM_BYTES = 16 * 1024 * 1024


def iota(shape, axis):
    return lax.broadcasted_iota(jnp.int32, shape, axis)


def slot_kernel(ids_ref, slot_ref):
    count = ids_ref.shape[1]
    cluster = jnp.broadcast_to(ids_ref[...] // 2, (count, count))
    above, here = iota((count, count), 0), iota((count, count), 1)
    cluster_above = jnp.sum(jnp.where(above == here, cluster, 0), axis=1, keepdims=True)
    earlier = (cluster_above == cluster) & (above < here)
    rank = jnp.sum(earlier.astype(jnp.int32), axis=0, keepdims=True)
    slot_ref[...] = cluster[:1] * CAPACITY + rank


def place_kernel(slot_ref, rows_ref, placed_ref):
    values = rows_ref[...].astype(jnp.float32)
    norm = lax.rsqrt(jnp.sum(values * values, axis=1, keepdims=True) + 1e-06)
    unit = (values * norm).astype(jnp.bfloat16)
    shape = (placed_ref.shape[0], rows_ref.shape[0])
    onehot = (iota(shape, 0) == slot_ref[...]).astype(jnp.float32).astype(jnp.bfloat16)
    placed_ref[...] = jnp.dot(onehot, unit, preferred_element_type=jnp.float32).astype(
        jnp.bfloat16
    )


def present(rows):
    return jnp.max(jnp.abs(rows).astype(jnp.float32), axis=1, keepdims=True) > 0


def scores_of(others, own):
    return lax.dot_general(
        others, own, (((1,), (1,)), ((), ())), preferred_element_type=jnp.float32
    )


def own_kernel(own_ref, best_ref):
    own = own_ref[...]
    scores = scores_of(own, own)
    allowed = present(own) & (iota(scores.shape, 0) != iota(scores.shape, 1))
    best_ref[...] = jnp.max(jnp.where(allowed, scores, LOWEST), axis=0, keepdims=True)


def turned(place, turn, chips):
    place = place + turn
    return jnp.where(place < chips, place, place - chips)


def cross_kernel(turn, own_ref, other_ref, best_ref, message_ref):
    own, other = own_ref[...], other_ref[...]
    scores = jnp.where(present(other), scores_of(other, own), LOWEST)
    best = jnp.maximum(best_ref[...], jnp.max(scores, axis=0, keepdims=True))
    shape = message_ref.shape
    source, lane = turned(iota(shape, 0), turn, shape[0]), iota(shape, 1)
    message = jnp.zeros(shape, jnp.float32)
    per_part = LANES // CAPACITY
    for part in range(best.shape[1] // LANES):
        mine = source == part * per_part + lane // CAPACITY
        message = jnp.where(mine, best[:, part * LANES : (part + 1) * LANES], message)
    message_ref[...] = message


def pick_kernel(turn, slot_ref, answers_ref, out_ref):
    slot = slot_ref[...]
    answers = answers_ref[...]
    count = slot.shape[1]
    chips = answers.shape[0]
    cluster = turned(iota((chips, count), 0), turn, chips)
    onehot = (cluster == slot // CAPACITY).astype(jnp.float32).astype(jnp.bfloat16)
    parts = []
    for _ in range(3):
        parts.append(answers.astype(jnp.bfloat16))
        answers = answers - parts[-1].astype(jnp.float32)
    found = lax.dot_general(
        jnp.concatenate(parts, axis=0),
        jnp.concatenate([onehot] * 3, axis=0),
        (((0,), (0,)), ((), ())),
        preferred_element_type=jnp.float32,
    )
    mine = iota(found.shape, 0) % CAPACITY == slot % CAPACITY
    out_ref[...] = jnp.sum(jnp.where(mine, found, 0.0), axis=0, keepdims=True)


def groups(first, chips):
    return [[2 * ((first + k) % chips) + core for k in range(chips)] for core in range(2)]


def call(kernel, outs, flops, *args):
    whole = pl.BlockSpec(memory_space=pltpu.VMEM)
    moved = sum(a.size * a.dtype.itemsize for a in args)
    return pl.pallas_call(
        kernel,
        out_shape=outs,
        in_specs=[whole] * len(args),
        out_specs=jax.tree.map(lambda _: whole, outs),
        compiler_params=pltpu.CompilerParams(vmem_limit_bytes=VMEM_BYTES),
        cost_estimate=pl.CostEstimate(flops=flops, bytes_accessed=moved, transcendentals=0),
    )(*args)


def body(embeddings, block_ids):
    count, width = embeddings.shape
    devices = lax.axis_size("dev")
    chips = devices // 2
    slots = chips * CAPACITY
    turn = (ANSWERS_FIRST - ROWS_FIRST) % chips

    def exchange(blocks, first):
        return lax.all_to_all(
            blocks, "dev", 0, 0, axis_index_groups=groups(first, chips), tiled=True
        )

    row = jax.ShapeDtypeStruct
    slot = call(
        slot_kernel, row((1, count), jnp.int32), SLOT_COST, block_ids.reshape(1, count)
    )
    placed = call(
        place_kernel,
        row((slots, width), jnp.bfloat16),
        2 * slots * count * width,
        slot,
        embeddings,
    )
    own = exchange(placed.reshape(chips, CAPACITY, width), ROWS_FIRST).reshape(slots, width)
    other = lax.ppermute(own, "dev", [(d, d ^ 1) for d in range(devices)])
    flops = 2 * slots * slots * width
    best = call(own_kernel, row((1, slots), jnp.float32), flops, own)
    cross = functools.partial(cross_kernel, turn)
    message = call(cross, row((chips, LANES), jnp.float32), flops, own, other, best)
    answers = exchange(message.reshape(chips, 1, LANES), ANSWERS_FIRST)
    answers = answers.reshape(chips, LANES)
    flops = 6 * chips * LANES * count
    pick = functools.partial(pick_kernel, turn)
    out = call(pick, row((1, count), jnp.float32), flops, slot, answers)
    return out.reshape(count)


def solution(mesh):
    placed = (P(("grp", "dev"), None), P(("grp", "dev")))
    return jax.shard_map(
        body, mesh=mesh, in_specs=placed, out_specs=P(("grp", "dev")), check_vma=False
    )
```

```python
import functools

import jax
import jax.numpy as jnp
from jax import lax
from jax.experimental import pallas as pl
from jax.experimental.pallas import tpu as pltpu
from jax.sharding import PartitionSpec as P

CAPACITY = 8
LANES = 128
LOWEST = -1e30
ROWS_FIRST = 42
ANSWERS_FIRST = 34
ORDER_COST = 10_000_000_000
SLOT_COST = 1_000_000
VMEM_BYTES = 16 * 1024 * 1024


def iota(shape, axis):
    return lax.broadcasted_iota(jnp.int32, shape, axis)


def order_kernel(same_ref, earlier_ref):
    above, here = iota(same_ref.shape, 0), iota(same_ref.shape, 1)
    same_ref[...] = (above == here).astype(jnp.int32)
    earlier_ref[...] = (above < here).astype(jnp.int32)


def slot_kernel(ids_ref, same_ref, earlier_ref, slot_ref):
    cluster = jnp.broadcast_to(ids_ref[...] // 2, same_ref.shape)
    cluster_above = jnp.sum(cluster * same_ref[...], axis=1, keepdims=True)
    earlier = jnp.where(cluster_above == cluster, earlier_ref[...], 0)
    rank = jnp.sum(earlier, axis=0, keepdims=True)
    slot_ref[...] = cluster[:1] * CAPACITY + rank


def place_kernel(slot_ref, rows_ref, placed_ref):
    values = rows_ref[...].astype(jnp.float32)
    norm = lax.rsqrt(jnp.sum(values * values, axis=1, keepdims=True) + 1e-06)
    unit = (values * norm).astype(jnp.bfloat16)
    shape = (placed_ref.shape[0], rows_ref.shape[0])
    onehot = (iota(shape, 0) == slot_ref[...]).astype(jnp.float32).astype(jnp.bfloat16)
    placed_ref[...] = jnp.dot(onehot, unit, preferred_element_type=jnp.float32).astype(
        jnp.bfloat16
    )


def present(rows):
    return jnp.max(jnp.abs(rows).astype(jnp.float32), axis=1, keepdims=True) > 0


def scores_of(others, own):
    return lax.dot_general(
        others, own, (((1,), (1,)), ((), ())), preferred_element_type=jnp.float32
    )


def own_kernel(own_ref, best_ref):
    own = own_ref[...]
    scores = scores_of(own, own)
    allowed = present(own) & (iota(scores.shape, 0) != iota(scores.shape, 1))
    best_ref[...] = jnp.max(jnp.where(allowed, scores, LOWEST), axis=0, keepdims=True)


def turned(place, turn, chips):
    place = place + turn
    return jnp.where(place < chips, place, place - chips)


def cross_kernel(turn, own_ref, other_ref, best_ref, message_ref):
    own, other = own_ref[...], other_ref[...]
    scores = jnp.where(present(other), scores_of(other, own), LOWEST)
    best = jnp.maximum(best_ref[...], jnp.max(scores, axis=0, keepdims=True))
    shape = message_ref.shape
    source, lane = turned(iota(shape, 0), turn, shape[0]), iota(shape, 1)
    message = jnp.zeros(shape, jnp.float32)
    per_part = LANES // CAPACITY
    for part in range(best.shape[1] // LANES):
        mine = source == part * per_part + lane // CAPACITY
        message = jnp.where(mine, best[:, part * LANES : (part + 1) * LANES], message)
    message_ref[...] = message


def pick_kernel(turn, slot_ref, answers_ref, out_ref):
    slot = slot_ref[...]
    answers = answers_ref[...]
    count = slot.shape[1]
    chips = answers.shape[0]
    cluster = turned(iota((chips, count), 0), turn, chips)
    onehot = (cluster == slot // CAPACITY).astype(jnp.float32).astype(jnp.bfloat16)
    parts = []
    for _ in range(3):
        parts.append(answers.astype(jnp.bfloat16))
        answers = answers - parts[-1].astype(jnp.float32)
    found = lax.dot_general(
        jnp.concatenate(parts, axis=0),
        jnp.concatenate([onehot] * 3, axis=0),
        (((0,), (0,)), ((), ())),
        preferred_element_type=jnp.float32,
    )
    mine = iota(found.shape, 0) % CAPACITY == slot % CAPACITY
    out_ref[...] = jnp.sum(jnp.where(mine, found, 0.0), axis=0, keepdims=True)


def groups(first, chips):
    return [[2 * ((first + k) % chips) + core for k in range(chips)] for core in range(2)]


def call(kernel, outs, flops, *args):
    whole = pl.BlockSpec(memory_space=pltpu.VMEM)
    moved = sum(a.size * a.dtype.itemsize for a in args)
    return pl.pallas_call(
        kernel,
        out_shape=outs,
        in_specs=[whole] * len(args),
        out_specs=jax.tree.map(lambda _: whole, outs),
        compiler_params=pltpu.CompilerParams(vmem_limit_bytes=VMEM_BYTES),
        cost_estimate=pl.CostEstimate(flops=flops, bytes_accessed=moved, transcendentals=0),
    )(*args)


def body(embeddings, block_ids):
    count, width = embeddings.shape
    devices = lax.axis_size("dev")
    chips = devices // 2
    slots = chips * CAPACITY
    turn = (ANSWERS_FIRST - ROWS_FIRST) % chips

    def exchange(blocks, first):
        return lax.all_to_all(
            blocks, "dev", 0, 0, axis_index_groups=groups(first, chips), tiled=True
        )

    row = jax.ShapeDtypeStruct
    square = row((count, count), jnp.int32)
    masks = call(order_kernel, (square, square), ORDER_COST)
    slot = call(
        slot_kernel, row((1, count), jnp.int32), SLOT_COST, block_ids.reshape(1, count), *masks
    )
    placed = call(
        place_kernel,
        row((slots, width), jnp.bfloat16),
        2 * slots * count * width,
        slot,
        embeddings,
    )
    own = exchange(placed.reshape(chips, CAPACITY, width), ROWS_FIRST).reshape(slots, width)
    other = lax.ppermute(own, "dev", [(d, d ^ 1) for d in range(devices)])
    flops = 2 * slots * slots * width
    best = call(own_kernel, row((1, slots), jnp.float32), flops, own)
    cross = functools.partial(cross_kernel, turn)
    message = call(cross, row((chips, LANES), jnp.float32), flops, own, other, best)
    answers = exchange(message.reshape(chips, 1, LANES), ANSWERS_FIRST)
    answers = answers.reshape(chips, LANES)
    flops = 6 * chips * LANES * count
    pick = functools.partial(pick_kernel, turn)
    out = call(pick, row((1, count), jnp.float32), flops, slot, answers)
    return out.reshape(count)


def solution(mesh):
    placed = (P(("grp", "dev"), None), P(("grp", "dev")))
    return jax.shard_map(
        body, mesh=mesh, in_specs=placed, out_specs=P(("grp", "dev")), check_vma=False
    )
```

```python
import functools

import jax
import jax.numpy as jnp
from jax import lax
from jax.experimental import pallas as pl
from jax.experimental.pallas import tpu as pltpu
from jax.sharding import PartitionSpec as P

CAPACITY = 8
LANES = 128
LOWEST = -1e30
ROWS_FIRST = 47
ANSWERS_FIRST = 34
ORDER_COST = 10_000_000_000
VMEM_BYTES = 16 * 1024 * 1024


def iota(shape, axis):
    return lax.broadcasted_iota(jnp.int32, shape, axis)


def order_kernel(same_ref, earlier_ref):
    above, here = iota(same_ref.shape, 0), iota(same_ref.shape, 1)
    same_ref[...] = (above == here).astype(jnp.int32)
    earlier_ref[...] = (above < here).astype(jnp.int32)


def place_kernel(ids_ref, same_ref, earlier_ref, rows_ref, placed_ref, slot_ref):
    cluster = jnp.broadcast_to(ids_ref[...] // 2, same_ref.shape)
    cluster_above = jnp.sum(cluster * same_ref[...], axis=1, keepdims=True)
    earlier = jnp.where(cluster_above == cluster, earlier_ref[...], 0)
    rank = jnp.sum(earlier, axis=0, keepdims=True)
    slot = cluster[:1] * CAPACITY + rank
    slot_ref[...] = slot
    values = rows_ref[...].astype(jnp.float32)
    norm = lax.rsqrt(jnp.sum(values * values, axis=1, keepdims=True) + 1e-06)
    unit = (values * norm).astype(jnp.bfloat16)
    shape = (placed_ref.shape[0], rows_ref.shape[0])
    onehot = (iota(shape, 0) == slot).astype(jnp.float32).astype(jnp.bfloat16)
    placed_ref[...] = jnp.dot(onehot, unit, preferred_element_type=jnp.float32).astype(
        jnp.bfloat16
    )


def present(rows):
    return jnp.max(jnp.abs(rows).astype(jnp.float32), axis=1, keepdims=True) > 0


def scores_of(others, own):
    return lax.dot_general(
        others, own, (((1,), (1,)), ((), ())), preferred_element_type=jnp.float32
    )


def own_kernel(own_ref, best_ref):
    own = own_ref[...]
    scores = scores_of(own, own)
    allowed = present(own) & (iota(scores.shape, 0) != iota(scores.shape, 1))
    best_ref[...] = jnp.max(jnp.where(allowed, scores, LOWEST), axis=0, keepdims=True)


def turned(place, turn, chips):
    place = place + turn
    return jnp.where(place < chips, place, place - chips)


def cross_kernel(turn, own_ref, other_ref, best_ref, message_ref):
    own, other = own_ref[...], other_ref[...]
    scores = jnp.where(present(other), scores_of(other, own), LOWEST)
    best = jnp.maximum(best_ref[...], jnp.max(scores, axis=0, keepdims=True))
    shape = message_ref.shape
    source, lane = turned(iota(shape, 0), turn, shape[0]), iota(shape, 1)
    message = jnp.zeros(shape, jnp.float32)
    per_part = LANES // CAPACITY
    for part in range(best.shape[1] // LANES):
        mine = source == part * per_part + lane // CAPACITY
        message = jnp.where(mine, best[:, part * LANES : (part + 1) * LANES], message)
    message_ref[...] = message


def pick_kernel(turn, slot_ref, answers_ref, out_ref):
    slot = slot_ref[...]
    answers = answers_ref[...]
    count = slot.shape[1]
    chips = answers.shape[0]
    cluster = turned(iota((chips, count), 0), turn, chips)
    onehot = (cluster == slot // CAPACITY).astype(jnp.float32).astype(jnp.bfloat16)
    parts = []
    for _ in range(3):
        parts.append(answers.astype(jnp.bfloat16))
        answers = answers - parts[-1].astype(jnp.float32)
    found = lax.dot_general(
        jnp.concatenate(parts, axis=0),
        jnp.concatenate([onehot] * 3, axis=0),
        (((0,), (0,)), ((), ())),
        preferred_element_type=jnp.float32,
    )
    mine = iota(found.shape, 0) % CAPACITY == slot % CAPACITY
    out_ref[...] = jnp.sum(jnp.where(mine, found, 0.0), axis=0, keepdims=True)


def groups(first, chips):
    return [[2 * ((first + k) % chips) + core for k in range(chips)] for core in range(2)]


def call(kernel, outs, flops, *args):
    whole = pl.BlockSpec(memory_space=pltpu.VMEM)
    moved = sum(a.size * a.dtype.itemsize for a in args)
    return pl.pallas_call(
        kernel,
        out_shape=outs,
        in_specs=[whole] * len(args),
        out_specs=jax.tree.map(lambda _: whole, outs),
        compiler_params=pltpu.CompilerParams(vmem_limit_bytes=VMEM_BYTES),
        cost_estimate=pl.CostEstimate(flops=flops, bytes_accessed=moved, transcendentals=0),
    )(*args)


def body(embeddings, block_ids):
    count, width = embeddings.shape
    devices = lax.axis_size("dev")
    chips = devices // 2
    slots = chips * CAPACITY
    turn = (ANSWERS_FIRST - ROWS_FIRST) % chips

    def exchange(blocks, first):
        return lax.all_to_all(
            blocks, "dev", 0, 0, axis_index_groups=groups(first, chips), tiled=True
        )

    row = jax.ShapeDtypeStruct
    square = row((count, count), jnp.int32)
    masks = call(order_kernel, (square, square), ORDER_COST)
    placed, slot = call(
        place_kernel,
        (row((slots, width), jnp.bfloat16), row((1, count), jnp.int32)),
        2 * slots * count * width,
        block_ids.reshape(1, count),
        *masks,
        embeddings,
    )
    own = exchange(placed.reshape(chips, CAPACITY, width), ROWS_FIRST).reshape(slots, width)
    other = lax.ppermute(own, "dev", [(d, d ^ 1) for d in range(devices)])
    flops = 2 * slots * slots * width
    best = call(own_kernel, row((1, slots), jnp.float32), flops, own)
    cross = functools.partial(cross_kernel, turn)
    message = call(cross, row((chips, LANES), jnp.float32), flops, own, other, best)
    answers = exchange(message.reshape(chips, 1, LANES), ANSWERS_FIRST)
    answers = answers.reshape(chips, LANES)
    flops = 6 * chips * LANES * count
    pick = functools.partial(pick_kernel, turn)
    out = call(pick, row((1, count), jnp.float32), flops, slot, answers)
    return out.reshape(count)


def solution(mesh):
    placed = (P(("grp", "dev"), None), P(("grp", "dev")))
    return jax.shard_map(
        body, mesh=mesh, in_specs=placed, out_specs=P(("grp", "dev")), check_vma=False
    )
```

```python
import functools

import jax
import jax.numpy as jnp
from jax import lax
from jax.experimental import pallas as pl
from jax.experimental.pallas import tpu as pltpu
from jax.sharding import PartitionSpec as P

CAPACITY = 8
LANES = 128
BLOCK = 256
LOWEST = -1e30
ROWS_FIRST = 47
ANSWERS_FIRST = 34
ORDER_COST = 10_000_000_000
VMEM_BYTES = 16 * 1024 * 1024


def iota(shape, axis):
    return lax.broadcasted_iota(jnp.int32, shape, axis)


def order_kernel(same_ref, earlier_ref):
    above, here = iota(same_ref.shape, 0), iota(same_ref.shape, 1)
    same_ref[...] = (above == here).astype(jnp.int32)
    earlier_ref[...] = (above < here).astype(jnp.int32)


def place_kernel(ids_ref, same_ref, earlier_ref, rows_ref, placed_ref, slot_ref):
    cluster = jnp.broadcast_to(ids_ref[...] // 2, same_ref.shape)
    cluster_above = jnp.sum(cluster * same_ref[...], axis=1, keepdims=True)
    earlier = jnp.where(cluster_above == cluster, earlier_ref[...], 0)
    rank = jnp.sum(earlier, axis=0, keepdims=True)
    slot = cluster[:1] * CAPACITY + rank
    slot_ref[...] = slot
    values = rows_ref[...].astype(jnp.float32)
    norm = lax.rsqrt(jnp.sum(values * values, axis=1, keepdims=True) + 1e-06)
    unit = (values * norm).astype(jnp.bfloat16)
    shape = (placed_ref.shape[0], rows_ref.shape[0])
    onehot = (iota(shape, 0) == slot).astype(jnp.float32).astype(jnp.bfloat16)
    placed_ref[...] = jnp.dot(onehot, unit, preferred_element_type=jnp.float32).astype(
        jnp.bfloat16
    )


def present(rows):
    return jnp.max(jnp.abs(rows).astype(jnp.float32), axis=1, keepdims=True) > 0


def scores_of(others, own):
    return lax.dot_general(
        others, own, (((1,), (1,)), ((), ())), preferred_element_type=jnp.float32
    )


def own_kernel(own_ref, best_ref):
    own = own_ref[...]
    scores = scores_of(own, own)
    allowed = present(own) & (iota(scores.shape, 0) != iota(scores.shape, 1))
    best_ref[...] = jnp.max(jnp.where(allowed, scores, LOWEST), axis=0, keepdims=True)


def turned(place, turn, chips):
    place = place + turn
    return jnp.where(place < chips, place, place - chips)


def cross_kernel(turn, own_ref, other_ref, best_ref, message_ref):
    own, other = own_ref[...], other_ref[...]
    usable = present(other)
    found = []
    for start in range(0, own.shape[0], BLOCK):
        scores = scores_of(other, own[start : start + BLOCK])
        found.append(jnp.max(jnp.where(usable, scores, LOWEST), axis=0, keepdims=True))
    best = jnp.maximum(best_ref[...], jnp.concatenate(found, axis=1))
    shape = message_ref.shape
    source, lane = turned(iota(shape, 0), turn, shape[0]), iota(shape, 1)
    message = jnp.zeros(shape, jnp.float32)
    per_part = LANES // CAPACITY
    for part in range(best.shape[1] // LANES):
        mine = source == part * per_part + lane // CAPACITY
        message = jnp.where(mine, best[:, part * LANES : (part + 1) * LANES], message)
    message_ref[...] = message


def pick_kernel(turn, slot_ref, answers_ref, out_ref):
    slot = slot_ref[...]
    answers = answers_ref[...]
    count = slot.shape[1]
    chips = answers.shape[0]
    cluster = turned(iota((chips, count), 0), turn, chips)
    onehot = (cluster == slot // CAPACITY).astype(jnp.float32).astype(jnp.bfloat16)
    parts = []
    for _ in range(3):
        parts.append(answers.astype(jnp.bfloat16))
        answers = answers - parts[-1].astype(jnp.float32)
    found = lax.dot_general(
        jnp.concatenate(parts, axis=0),
        jnp.concatenate([onehot] * 3, axis=0),
        (((0,), (0,)), ((), ())),
        preferred_element_type=jnp.float32,
    )
    mine = iota(found.shape, 0) % CAPACITY == slot % CAPACITY
    out_ref[...] = jnp.sum(jnp.where(mine, found, 0.0), axis=0, keepdims=True)


def groups(first, chips):
    return [[2 * ((first + k) % chips) + core for k in range(chips)] for core in range(2)]


def call(kernel, outs, flops, *args):
    whole = pl.BlockSpec(memory_space=pltpu.VMEM)
    moved = sum(a.size * a.dtype.itemsize for a in args)
    return pl.pallas_call(
        kernel,
        out_shape=outs,
        in_specs=[whole] * len(args),
        out_specs=jax.tree.map(lambda _: whole, outs),
        compiler_params=pltpu.CompilerParams(vmem_limit_bytes=VMEM_BYTES),
        cost_estimate=pl.CostEstimate(flops=flops, bytes_accessed=moved, transcendentals=0),
    )(*args)


def body(embeddings, block_ids):
    count, width = embeddings.shape
    devices = lax.axis_size("dev")
    chips = devices // 2
    slots = chips * CAPACITY
    turn = (ANSWERS_FIRST - ROWS_FIRST) % chips

    def exchange(blocks, first):
        return lax.all_to_all(
            blocks, "dev", 0, 0, axis_index_groups=groups(first, chips), tiled=True
        )

    row = jax.ShapeDtypeStruct
    square = row((count, count), jnp.int32)
    masks = call(order_kernel, (square, square), ORDER_COST)
    placed, slot = call(
        place_kernel,
        (row((slots, width), jnp.bfloat16), row((1, count), jnp.int32)),
        2 * slots * count * width,
        block_ids.reshape(1, count),
        *masks,
        embeddings,
    )
    own = exchange(placed.reshape(chips, CAPACITY, width), ROWS_FIRST).reshape(slots, width)
    other = lax.ppermute(own, "dev", [(d, d ^ 1) for d in range(devices)])
    flops = 2 * slots * slots * width
    best = call(own_kernel, row((1, slots), jnp.float32), flops, own)
    cross = functools.partial(cross_kernel, turn)
    message = call(cross, row((chips, LANES), jnp.float32), flops, own, other, best)
    answers = exchange(message.reshape(chips, 1, LANES), ANSWERS_FIRST)
    answers = answers.reshape(chips, LANES)
    flops = 6 * chips * LANES * count
    pick = functools.partial(pick_kernel, turn)
    out = call(pick, row((1, count), jnp.float32), flops, slot, answers)
    return out.reshape(count)


def solution(mesh):
    placed = (P(("grp", "dev"), None), P(("grp", "dev")))
    return jax.shard_map(
        body, mesh=mesh, in_specs=placed, out_specs=P(("grp", "dev")), check_vma=False
    )
```
